32 devices in a mesh: dp: 8 (over y, x, core), seq: 4 (over z).
Axes of the slice: x: 2, y: 2, z: 4, core: 2. Of those that a mesh axis runs over, the one named last changes fastest.
Arguments:
- queries: bfloat16 [5120, 768], P(('dp', 'seq')), may hold values from -8 to 8
- keys: bfloat16 [5120, 768], P(('dp', 'seq')), may hold values from -8 to 8
- values: bfloat16 [5120, 768], P(('dp', 'seq')), may hold values from -6 to 6
- frames: bfloat16 [5120, 768], P(('dp', 'seq')), may hold values from -4 to 4
- upstream: bfloat16 [5120, 768], P(('dp', 'seq')), may hold values from -6 to 6
- lengths: int32 [8], P('dp'), may hold values from 160 to 640, as said below
- conv_kernel: bfloat16 [32, 768], replicated, may hold values from -1 to 1
Outputs:
- out: bfloat16 [5120, 768], P(('dp', 'seq'))
- query_grad: bfloat16 [5120, 768], P(('dp', 'seq'))
- key_grad: bfloat16 [5120, 768], P(('dp', 'seq'))
- value_grad: bfloat16 [5120, 768], P(('dp', 'seq'))
- frame_grad: bfloat16 [5120, 768], P(('dp', 'seq'))
- kernel_grad: float32 [32, 768], replicated
The draws below stay inside these ranges and needn't reach their ends.
Inputs may be any that keep to these rules, and one draw needn't show every extreme that they name: `lengths`: one utterance has all 640 frames live and another has 160.
All inputs are finite; a program needn't handle non-finite values.
Results may differ from the reference program's by a relative error of at most 0.0262.
Values may be sent and summed in bfloat16 or wider, within the bound.
A program may use at most 128 MiB of HBM per device.

```python
import jax
import jax.numpy as jnp
from jax import lax

HEADS = 12
HEAD_DIM = 64
CHANNELS = 768
KERNEL = 32
UTTS = 8
SEQLEN = 640
TOKENS = 5120


def paired_rows(key):
    base_key = jax.random.fold_in(key, 7001)
    query_key = jax.random.fold_in(base_key, 1)
    key_key = jax.random.fold_in(base_key, 2)
    query_rows = jnp.clip(1.5 * jax.random.normal(query_key, (TOKENS, CHANNELS), jnp.float32), -6.0, 6.0)
    key_rows = jnp.clip(1.5 * jax.random.normal(key_key, (TOKENS, CHANNELS), jnp.float32), -6.0, 6.0)
    return (query_rows, key_rows)


def draw_queries(key, part):
    return paired_rows(key)[0].astype(jnp.bfloat16)


def draw_keys(key, part):
    return paired_rows(key)[1].astype(jnp.bfloat16)


def draw_lengths(key, part):
    length_key = jax.random.fold_in(key, 9001)
    drawn = jax.random.randint(jax.random.fold_in(length_key, 1), (UTTS,), SEQLEN // 4, SEQLEN + 1)
    order = jax.random.permutation(jax.random.fold_in(length_key, 2), UTTS)
    drawn = drawn.at[order[0]].set(SEQLEN)
    drawn = drawn.at[order[1]].set(SEQLEN // 4)
    return drawn.astype(jnp.int32)


def level_of(rng, dims, pieces, low, top_value):
    def one(axis_at, blocks):
        steps = jax.random.uniform(jax.random.fold_in(jax.random.fold_in(rng, 6), axis_at), (blocks,), jnp.float32, low / len(pieces), top_value / len(pieces))
        return jnp.repeat(jnp.exp(steps), dims[axis_at] // blocks).reshape((-1,) + (1,) * (len(dims) - axis_at - 1))

    factor_of = one(*pieces[0])
    for cut in pieces[1:]:
        factor_of = factor_of * one(*cut)
    return factor_of


def centred(stream_key, dims, deviation, most, cuts=(), kind=jnp.bfloat16):
    factor_of = level_of(stream_key, dims, cuts, -0.22, 0.18) if cuts else 1.0
    values = jax.random.normal(stream_key, dims, jnp.float32) * deviation * factor_of
    return jnp.minimum(jnp.maximum(values, -most), most).astype(kind)


def setup_inputs(seed: int = 0) -> dict:
    seeds = jax.random.split(jax.random.key(seed), 8)
    queries = draw_queries(jax.random.fold_in(seeds[7], 71), 0)
    keys = draw_keys(jax.random.fold_in(seeds[7], 71), 0)
    values = centred(seeds[2], (TOKENS, CHANNELS), 1.0, 6.0, ((0, 32),))
    frames = centred(seeds[3], (TOKENS, CHANNELS), 0.5, 4.0, ((0, 32),))
    upstream = centred(seeds[4], (TOKENS, CHANNELS), 1.0, 6.0, ((0, 32),))
    lengths = draw_lengths(jax.random.fold_in(seeds[7], 71), 0)
    conv_kernel = centred(seeds[6], (KERNEL, CHANNELS), KERNEL ** -0.5, 1.0)
    return {"queries": queries, "keys": keys, "values": values, "frames": frames, "upstream": upstream, "lengths": lengths, "conv_kernel": conv_kernel}


def split_heads(flat_array):
    return flat_array.reshape(SEQLEN, HEADS, HEAD_DIM).transpose(1, 0, 2)


def merge_heads(head_array):
    return head_array.transpose(1, 0, 2).reshape(SEQLEN, CHANNELS)


def utterance_pass(queries, keys, values, frames, upstream, length, weights):
    score_scale = HEAD_DIM ** -0.5
    positions = jnp.arange(SEQLEN, dtype=jnp.int32)
    key_live = positions < length
    frame_live = key_live[:, None]

    def head_scores(query_head, key_head):
        scores = jnp.dot(query_head, key_head.T, preferred_element_type=jnp.float32) * score_scale
        return jnp.where(key_live[None, :], scores, -jnp.inf)

    def forward_head(head_items):
        query_head, key_head, value_head = head_items
        scores = head_scores(query_head, key_head)
        running_top = jnp.max(scores, axis=1)
        log_total = running_top + jnp.log(jnp.sum(jnp.exp(scores - running_top[:, None]), axis=1))
        prob_bf = jnp.exp(scores - log_total[:, None]).astype(jnp.bfloat16)
        attended_head = jnp.dot(prob_bf, value_head, preferred_element_type=jnp.float32).astype(jnp.bfloat16)
        return attended_head, log_total

    query_heads = split_heads(queries)
    key_heads = split_heads(keys)
    value_heads = split_heads(values)
    attended_heads, log_totals = lax.map(forward_head, (query_heads, key_heads, value_heads))
    attended = merge_heads(attended_heads)
    hidden = (frames.astype(jnp.float32) + attended.astype(jnp.float32)).astype(jnp.bfloat16)
    masked = jnp.where(frame_live, hidden, jnp.zeros_like(hidden)).astype(jnp.float32)
    padded = jnp.concatenate([jnp.zeros((KERNEL - 1, CHANNELS), jnp.float32), masked], axis=0)
    conv_out = jnp.zeros((SEQLEN, CHANNELS), jnp.float32)
    for tap_index in range(KERNEL):
        conv_out = conv_out + weights[tap_index] * padded[KERNEL - 1 - tap_index:KERNEL - 1 - tap_index + SEQLEN]
    sig_conv = jax.nn.sigmoid(conv_out)
    out = (hidden.astype(jnp.float32) + conv_out * sig_conv).astype(jnp.bfloat16)
    loss_grad = jnp.where(frame_live, upstream.astype(jnp.float32), 0.0)
    conv_rounded = (loss_grad * sig_conv * (1.0 + conv_out * (1.0 - sig_conv))).astype(jnp.bfloat16)
    conv_grad = lax.optimization_barrier(conv_rounded).astype(jnp.float32)
    kernel_terms = jnp.stack([jnp.sum(conv_grad * padded[KERNEL - 1 - tap_index:KERNEL - 1 - tap_index + SEQLEN], axis=0) for tap_index in range(KERNEL)])
    ahead_rows = jnp.concatenate([conv_grad, jnp.zeros((KERNEL - 1, CHANNELS), jnp.float32)], axis=0)
    back_conv = jnp.zeros((SEQLEN, CHANNELS), jnp.float32)
    for tap_index in range(KERNEL):
        back_conv = back_conv + weights[tap_index] * ahead_rows[tap_index:tap_index + SEQLEN]
    frame_grad = (loss_grad + jnp.where(frame_live, back_conv, 0.0)).astype(jnp.bfloat16)
    grad_heads = split_heads(frame_grad)
    delta_rows = jnp.sum(grad_heads.astype(jnp.float32) * attended_heads.astype(jnp.float32), axis=2)

    def backward_head(head_items):
        query_head, key_head, value_head, grad_head, log_total, delta_head = head_items
        scores = head_scores(query_head, key_head)
        soft_weights = jnp.exp(scores - log_total[:, None])
        prob_bf = soft_weights.astype(jnp.bfloat16)
        prob_grad = jnp.dot(grad_head, value_head.T, preferred_element_type=jnp.float32)
        score_grad = (soft_weights * (prob_grad - delta_head[:, None])).astype(jnp.bfloat16)
        query_part = (jnp.dot(score_grad, key_head, preferred_element_type=jnp.float32) * score_scale).astype(jnp.bfloat16)
        key_part = (jnp.dot(score_grad.T, query_head, preferred_element_type=jnp.float32) * score_scale).astype(jnp.bfloat16)
        value_part = jnp.dot(prob_bf.T, grad_head, preferred_element_type=jnp.float32).astype(jnp.bfloat16)
        return query_part, key_part, value_part

    query_grads, key_grads, value_grads = lax.map(backward_head, (query_heads, key_heads, value_heads, grad_heads, log_totals, delta_rows))
    return out, merge_heads(query_grads), merge_heads(key_grads), merge_heads(value_grads), frame_grad, kernel_terms


def reference(queries, keys, values, frames, upstream, lengths, conv_kernel):
    weights = conv_kernel.astype(jnp.float32)
    stacked_shape = (UTTS, SEQLEN, CHANNELS)

    def per_utterance(utt_items):
        return utterance_pass(utt_items[0], utt_items[1], utt_items[2], utt_items[3], utt_items[4], utt_items[5], weights)

    results = lax.map(per_utterance, (queries.reshape(stacked_shape), keys.reshape(stacked_shape), values.reshape(stacked_shape), frames.reshape(stacked_shape), upstream.reshape(stacked_shape), lengths))
    out, query_grad, key_grad, value_grad, frame_grad, kernel_terms = results
    kernel_grad = jnp.sum(kernel_terms, axis=0) / UTTS
    full_shape = (TOKENS, CHANNELS)
    return (out.reshape(full_shape), query_grad.reshape(full_shape), key_grad.reshape(full_shape), value_grad.reshape(full_shape), frame_grad.reshape(full_shape), kernel_grad)
```

```python
import functools

import jax
import jax.numpy as jnp
from jax import lax
from jax.experimental import pallas as pl
from jax.experimental.pallas import tpu as pltpu
from jax.sharding import PartitionSpec as P

HEAD_DIM = 64
KERNEL = 32


def shifted(x, axis, by):
    count = lax.axis_size(axis)
    pairs = [(i, i + by) for i in range(count) if 0 <= i + by < count]
    return lax.ppermute(x, axis, pairs)


def per_device(queries, keys, values, frames, upstream, lengths, conv_kernel):
    row_count = queries.shape[0]
    channels = queries.shape[1]
    head_count = channels // HEAD_DIM
    seq_count = lax.axis_size("seq")
    first_row = lax.axis_index("seq") * row_count
    length = lengths[0]
    score_scale = HEAD_DIM ** (-0.5)
    span = row_count * seq_count
    shards = 1
    while shards * row_count < 512 and seq_count % (2 * shards) == 0:
        shards = shards * 2
    key_block = row_count * shards
    block_count = span // key_block
    key_all, value_all = (
        lax.all_gather(keys, "seq", axis=0, tiled=True),
        lax.all_gather(values, "seq", axis=0, tiled=True),
    )
    key_blocks = key_all.reshape(block_count, key_block, head_count, HEAD_DIM)
    value_blocks = value_all.reshape(block_count, key_block, head_count, HEAD_DIM)
    block_starts = jnp.arange(block_count, dtype=jnp.int32) * key_block
    query_heads = queries.reshape(row_count, head_count, HEAD_DIM)

    def block_scores(key_part, block_start):
        scores = (
            jnp.einsum("thd,khd->htk", query_heads, key_part, preferred_element_type=jnp.float32)
            * score_scale
        )
        key_live = block_start + jnp.arange(key_part.shape[0], dtype=jnp.int32) < length
        return jnp.where(key_live[None, None, :], scores, -jnp.inf)

    def running_total(state_pair, block_items):
        running_top, total_sum = state_pair
        key_part, block_start = block_items
        scores = block_scores(key_part, block_start)
        higher = jnp.maximum(running_top, jnp.max(scores, axis=2))
        total_sum = total_sum * jnp.exp(running_top - higher) + jnp.sum(
            jnp.exp(scores - higher[:, :, None]), axis=2
        )
        return ((higher, total_sum), None)

    start_state = (
        jnp.full((head_count, row_count), -1e30, jnp.float32),
        jnp.zeros((head_count, row_count), jnp.float32),
    )
    (running_top, total_sum), unused = lax.scan(
        running_total, start_state, (key_blocks, block_starts)
    )
    log_total = running_top + jnp.log(total_sum)

    def attend_block(attend_acc, block_items):
        key_part, value_part, block_start = block_items
        prob_bf = jnp.exp(block_scores(key_part, block_start) - log_total[:, :, None]).astype(
            jnp.bfloat16
        )
        return (
            attend_acc
            + jnp.einsum("htk,khd->thd", prob_bf, value_part, preferred_element_type=jnp.float32),
            None,
        )

    attend_acc, unused = lax.scan(
        attend_block,
        jnp.zeros((row_count, head_count, HEAD_DIM), jnp.float32),
        (key_blocks, value_blocks, block_starts),
    )
    attended = attend_acc.reshape(row_count, channels).astype(jnp.bfloat16)
    frame_live = (first_row + jnp.arange(row_count, dtype=jnp.int32) < length)[:, None]
    hidden = (frames.astype(jnp.float32) + attended.astype(jnp.float32)).astype(jnp.bfloat16)
    masked = jnp.where(frame_live, hidden, jnp.zeros_like(hidden))
    past_rows = shifted(masked[row_count - (KERNEL - 1) :], "seq", 1)
    extended = jnp.concatenate([past_rows, masked], axis=0).astype(jnp.float32)
    weights = conv_kernel.astype(jnp.float32)
    conv_out = jnp.zeros((row_count, channels), jnp.float32)
    for tap_index in range(KERNEL):
        conv_out = (
            conv_out
            + weights[tap_index]
            * extended[KERNEL - 1 - tap_index : KERNEL - 1 - tap_index + row_count]
        )
    sig_conv = jax.nn.sigmoid(conv_out)
    out = (hidden.astype(jnp.float32) + conv_out * sig_conv).astype(jnp.bfloat16)
    loss_grad = jnp.where(frame_live, upstream.astype(jnp.float32), 0.0)
    conv_grad = (loss_grad * sig_conv * (1.0 + conv_out * (1.0 - sig_conv))).astype(jnp.bfloat16)
    conv_float = conv_grad.astype(jnp.float32)
    kernel_part = jnp.stack(
        [
            jnp.sum(
                conv_float * extended[KERNEL - 1 - tap_index : KERNEL - 1 - tap_index + row_count],
                axis=0,
            )
            for tap_index in range(KERNEL)
        ]
    )
    future_rows = shifted(conv_grad[: KERNEL - 1], "seq", -1)
    ahead_rows = jnp.concatenate([conv_grad, future_rows], axis=0).astype(jnp.float32)
    back_conv = jnp.zeros((row_count, channels), jnp.float32)
    for tap_index in range(KERNEL):
        back_conv = back_conv + weights[tap_index] * ahead_rows[tap_index : tap_index + row_count]
    frame_grad = (loss_grad + jnp.where(frame_live, back_conv, 0.0)).astype(jnp.bfloat16)
    grad_heads = frame_grad.reshape(row_count, head_count, HEAD_DIM)
    attended_heads = attended.reshape(row_count, head_count, HEAD_DIM)
    delta_rows = jnp.sum(
        grad_heads.astype(jnp.float32) * attended_heads.astype(jnp.float32), axis=2
    ).T

    def score_grads(key_part, value_part, block_start):
        soft_weights = jnp.exp(block_scores(key_part, block_start) - log_total[:, :, None])
        prob_grad = jnp.einsum(
            "thd,khd->htk", grad_heads, value_part, preferred_element_type=jnp.float32
        )
        score_grad = (soft_weights * (prob_grad - delta_rows[:, :, None])).astype(jnp.bfloat16)
        return (soft_weights.astype(jnp.bfloat16), score_grad)

    def gradient_block(query_acc, block_items):
        key_part, value_part, block_start = block_items
        prob_bf, score_grad = score_grads(key_part, value_part, block_start)
        query_acc = query_acc + jnp.einsum(
            "htk,khd->thd", score_grad, key_part, preferred_element_type=jnp.float32
        )
        key_term = (
            jnp.einsum("htk,thd->khd", score_grad, query_heads, preferred_element_type=jnp.float32)
            * score_scale
        )
        value_term = jnp.einsum(
            "htk,thd->khd", prob_bf, grad_heads, preferred_element_type=jnp.float32
        )
        grad_terms = jnp.concatenate(
            [key_term.reshape(key_block, channels), value_term.reshape(key_block, channels)], axis=1
        )
        return (query_acc, grad_terms)

    query_acc, grad_terms = lax.scan(
        gradient_block,
        jnp.zeros((row_count, head_count, HEAD_DIM), jnp.float32),
        (key_blocks, value_blocks, block_starts),
    )
    own_rows = lax.psum_scatter(
        grad_terms.reshape(span, 2 * channels).astype(jnp.bfloat16),
        "seq",
        scatter_dimension=0,
        tiled=True,
    ).astype(jnp.float32)
    key_grad = own_rows[:, :channels].astype(jnp.bfloat16)
    value_grad = own_rows[:, channels:].astype(jnp.bfloat16)
    query_grad = (query_acc * score_scale).reshape(row_count, channels).astype(jnp.bfloat16)
    kernel_total = lax.psum(kernel_part, ("dp", "seq"))
    kernel_grad = kernel_total / lax.axis_size("dp")
    return (out, query_grad, key_grad, value_grad, frame_grad, kernel_grad)


BF = jnp.bfloat16
F32 = jnp.float32
MESH = pl.DeviceIdType.MESH
NEG = float("-inf")
Q, K, V, F, U = range(5)
OUT, FG, DQ, DK, DV = range(5)


def dot(a, b, dims=((1,), (0,))):
    return lax.dot_general(a, b, (dims, ((), ())), preferred_element_type=F32)


def side(a, b):
    return jnp.concatenate([a, b], axis=1)


def stack(*parts):
    return jnp.concatenate(parts, axis=0)


def main_kernel(
    n_dp, len_ref, q_ref, k_ref, v_ref, f_ref, u_ref, w_ref, out_a, out_b, out_g,
    send_a, send_b, x_a, recv_b, q_b, k_b, v_b, f_b, u_b, o_a, o_b, p_scr, s_scr, ds_scr,
    att_t, r_scr, hid, m_a, m_b, c_a, c_b, w_scr, kg_acc, kg_own, kg_recv, kg_tot,
    in_send, in_recv, back_send, back_recv, kg_send, kg_rsem, kt_send, kt_rsem,
):
    rows = q_ref.shape[0]
    half = rows // 2
    span = 4 * rows
    mid = span // 2
    me = lax.axis_index("seq")
    dp = lax.axis_index("dp")
    length = len_ref[0]

    barrier = pltpu.get_barrier_semaphore()
    for j in range(1, 4):
        pl.semaphore_signal(barrier, inc=1, device_id={"seq": lax.rem(me + j, 4)}, device_id_type=MESH)
    for j in range(1, n_dp):
        pl.semaphore_signal(barrier, inc=1, device_id={"dp": lax.rem(dp + j, n_dp)}, device_id_type=MESH)

    inputs = (q_ref, k_ref, v_ref, f_ref, u_ref)
    my_rows = pl.ds(pl.multiple_of(me * rows, rows), rows)

    def pack_in(n):
        ref = inputs[n]
        for d in range(4):
            send_a[n, d] = ref[:, 128 * d : 128 * d + 128]
            lanes = slice(512 + 64 * d, 512 + 64 * d + 64)
            send_b[n, d] = side(ref[0:half, lanes], ref[half:rows, lanes])
        x_a[n, my_rows, :] = send_a[n, me]
        recv_b[n, me] = send_b[n, me]

    def in_copy(n, part, j):
        dest = lax.rem(me + j, 4)
        if part == 0:
            src, dst = send_a.at[n, dest], x_a.at[n, my_rows, :]
        else:
            src, dst = send_b.at[n, dest], recv_b.at[n, me]
        return pltpu.make_async_remote_copy(
            src_ref=src, dst_ref=dst, send_sem=in_send.at[n, part, j - 1], recv_sem=in_recv.at[n, part, j - 1],
            device_id={"seq": dest}, device_id_type=MESH,
        )

    def back_copy(n, part, j):
        dest = lax.rem(me + j, 4)
        if part == 0:
            src = o_a.at[n, pl.ds(pl.multiple_of(dest * rows, rows), rows), :]
            dst = out_a.at[n, me]
        else:
            src, dst = o_b.at[n, dest], out_b.at[n, me]
        return pltpu.make_async_remote_copy(
            src_ref=src, dst_ref=dst, send_sem=back_send.at[n, part, j - 1], recv_sem=back_recv.at[n, part, j - 1],
            device_id={"seq": dest}, device_id_type=MESH,
        )

    def each(make, n, part, act):
        for j in (2, 1, 3):
            copy = make(n, part, j)
            if act == "start":
                copy.start()
            elif act == "recv":
                copy.wait_recv()
            else:
                copy.wait_send()

    pack_in(Q)
    pack_in(K)
    pl.semaphore_wait(barrier, 3 + n_dp - 1)
    each(in_copy, Q, 0, "start")
    each(in_copy, K, 0, "start")
    pack_in(V)
    each(in_copy, V, 0, "start")
    for n in (Q, K, V):
        each(in_copy, n, 1, "start")
    for n in (F, U):
        pack_in(n)
        each(in_copy, n, 0, "start")
    for n in (F, U):
        each(in_copy, n, 1, "start")

    w_scr[0] = w_ref[:, pl.ds(pl.multiple_of(me * 128, 128), 128)].astype(F32)
    pair = w_ref[:, pl.ds(pl.multiple_of(512 + (me // 2) * 128, 128), 128)].astype(F32)
    single = jnp.where(lax.rem(me, 2) == 0, pair, side(pair[:, 64:], pair[:, :64]))
    w_scr[1] = side(single[:, :64], single[:, :64])
    kg_acc[...] = jnp.zeros_like(kg_acc)

    chunk = mid
    lane = lax.broadcasted_iota(jnp.int32, (span, 128), 1)
    first_head = lane < 64

    def pick(x, head):
        return jnp.where(first_head if head == 0 else ~first_head, x, jnp.zeros_like(x))

    def forward(slot, key_ref, query, value_t):
        top = None
        for c in range(span // chunk):
            s = dot(key_ref[c * chunk : (c + 1) * chunk, :], query, ((1,), (1,)))
            live = c * chunk + lax.broadcasted_iota(jnp.int32, (chunk, 1), 0) < length
            s = jnp.where(live, s, NEG)
            s_scr[c * chunk : (c + 1) * chunk, :] = s
            here = jnp.max(s, axis=0, keepdims=True)
            top = here if top is None else jnp.maximum(top, here)
        total = None
        for c in range(span // chunk):
            p = jnp.exp(s_scr[c * chunk : (c + 1) * chunk, :] - top)
            here = jnp.sum(p, axis=0, keepdims=True)
            total = here if total is None else total + here
            p_scr[slot, c * chunk : (c + 1) * chunk, :] = p.astype(BF)
        scale = 1.0 / total
        r_scr[slot] = jnp.broadcast_to(scale, (8, span))
        att = (dot(value_t, p_scr[slot]) * scale).astype(BF).astype(F32)
        att_t[slot] = att
        return att

    def backward(slot, value_ref, grad_t, grad, query, key_t, delta):
        dk_parts, dv_parts = [], []
        for c in range(span // chunk):
            here = slice(c * chunk, (c + 1) * chunk)
            dprob = dot(value_ref[here, :], grad_t)
            p = p_scr[slot, here, :]
            ds = (p.astype(F32) * (dprob - delta)).astype(BF)
            ds_scr[here, :] = ds
            dk_parts.append(dot(ds, query))
            dv_parts.append(dot(p, grad))
        dq_t = dot(key_t, ds_scr[...])
        return dq_t, stack(*dk_parts), stack(*dv_parts)

    for n in (Q, K, V):
        each(in_copy, n, 0, "recv")
    value_t = jnp.transpose(x_a[V].astype(F32)).astype(BF)
    query = x_a[Q] * jnp.asarray(0.125, BF)
    atts = [forward(h, x_a.at[K], pick(query, h), value_t[64 * h : 64 * h + 64]) for h in range(2)]
    hid[0] = jnp.transpose(stack(*atts))

    for n, ref in ((Q, q_b), (K, k_b), (V, v_b)):
        each(in_copy, n, 1, "recv")
        for d in range(4):
            block = recv_b[n, d]
            ref[d * rows : d * rows + half, :] = block[:, :64]
            ref[d * rows + half : (d + 1) * rows, :] = block[:, 64:]
    value_tb = jnp.transpose(v_b[...].astype(F32)).astype(BF)
    query_b = q_b[...] * jnp.asarray(0.125, BF)
    att_b = jnp.transpose(forward(2, k_b, query_b, value_tb))
    hid[1, 0:mid, :] = side(att_b[:mid], att_b[mid:])

    tile = half

    def live_of(group, t0):
        t = t0 + lax.broadcasted_iota(jnp.int32, (tile, 128), 0)
        if group:
            t = t + jnp.where(lax.broadcasted_iota(jnp.int32, (tile, 128), 1) >= 64, mid, 0)
        return t < length

    def conv_group(group, f_in, u_in, m_ref, c_ref, out_ref, fg_ref):
        size = mid if group else span
        steps = size // tile

        def at(i):
            return pl.multiple_of(i * tile, tile)

        def fill(i, carry):
            t0 = at(i)
            here = pl.ds(t0, tile)
            hidden = (f_in[here, :].astype(F32) + hid[group, here, :]).astype(BF).astype(F32)
            hid[group, here, :] = hidden
            m_ref[pl.ds(t0 + 32, tile), :] = jnp.where(live_of(group, t0), hidden, 0.0)
            return carry

        lax.fori_loop(0, steps, fill, 0)
        zeros = jnp.zeros((32, 128), F32)
        if group:
            m_ref[0:32, :] = side(zeros[:, :64], m_ref[size : size + 32, :][:, :64])
        else:
            m_ref[0:32, :] = zeros

        def ahead(i, carry):
            t0 = at(i)
            here = pl.ds(t0, tile)
            conv = jnp.zeros((tile, 128), F32)
            for b in range(8):
                win = m_ref[pl.ds(t0 + 8 - b, tile + 24), :]
                for a in range(4):
                    tap = 8 * a + b
                    conv = conv + w_scr[group, tap : tap + 1, :] * win[24 - 8 * a : 24 - 8 * a + tile]
            sig = jax.nn.sigmoid(conv)
            out_ref[here, :] = (hid[group, here, :] + conv * sig).astype(BF)
            loss = jnp.where(live_of(group, t0), u_in[here, :].astype(F32), 0.0)
            cg = (loss * sig * (1.0 + conv * (1.0 - sig))).astype(BF).astype(F32)
            c_ref[here, :] = cg
            for b in range(8):
                win = m_ref[pl.ds(t0 + 8 - b, tile + 24), :]
                for a in range(4):
                    prod = cg * win[24 - 8 * a : 24 - 8 * a + tile]
                    kg_acc[group, 8 * a + b] += jnp.sum(prod.reshape(tile // 8, 8, 128), axis=0)
            return carry

        lax.fori_loop(0, steps, ahead, 0)
        if group:
            c_ref[size : size + 32, :] = side(c_ref[0:32, :][:, 64:], zeros[:, :64])
        else:
            c_ref[size : size + 32, :] = zeros

        def behind(i, carry):
            t0 = at(i)
            here = pl.ds(t0, tile)
            back = jnp.zeros((tile, 128), F32)
            for b in range(8):
                win = c_ref[pl.ds(t0 + b, tile + 24), :]
                for a in range(4):
                    tap = 8 * a + b
                    back = back + w_scr[group, tap : tap + 1, :] * win[8 * a : 8 * a + tile]
            loss = u_in[here, :].astype(F32) + back
            fg_ref[here, :] = jnp.where(live_of(group, t0), loss, 0.0).astype(BF)
            return carry

        lax.fori_loop(0, steps, behind, 0)

    def give_a(n):
        out_a[n, me] = o_a[n, my_rows, :]
        each(back_copy, n, 0, "start")

    def give_b(n):
        out_b[n, me] = o_b[n, me]
        each(back_copy, n, 1, "start")

    for n in (F, U):
        each(in_copy, n, 0, "recv")
    conv_group(0, x_a.at[F], x_a.at[U], m_a, c_a, o_a.at[OUT], o_a.at[FG])
    give_a(OUT)
    give_a(FG)

    for n, ref in ((F, f_b), (U, u_b)):
        each(in_copy, n, 1, "recv")
        for d in range(2):
            lo, hi = recv_b[n, d], recv_b[n, d + 2]
            ref[d * rows : d * rows + half, :] = side(lo[:, :64], hi[:, :64])
            ref[d * rows + half : (d + 1) * rows, :] = side(lo[:, 64:], hi[:, 64:])
    conv_group(1, f_b, u_b, m_b, c_b, f_b, u_b)
    for n, ref in ((OUT, f_b), (FG, u_b)):
        for d in range(2):
            top, low = ref[d * rows : d * rows + half, :], ref[d * rows + half : (d + 1) * rows, :]
            o_b[n, d] = side(top[:, :64], low[:, :64])
            o_b[n, d + 2] = side(top[:, 64:], low[:, 64:])
        give_b(n)

    sum_a = jnp.sum(kg_acc[0], axis=1)
    sum_b = jnp.sum(kg_acc[1], axis=1)
    kg_own[0] = sum_a
    kg_own[1] = sum_b + side(sum_b[:, 64:], sum_b[:, :64])
    kg_recv[dp] = kg_own[...]

    def kg_copy(j):
        dest = lax.rem(dp + j, n_dp)
        return pltpu.make_async_remote_copy(
            src_ref=kg_own, dst_ref=kg_recv.at[dp], send_sem=kg_send.at[j - 1], recv_sem=kg_rsem.at[j - 1],
            device_id={"dp": dest}, device_id_type=MESH,
        )

    def kt_copy(j):
        return pltpu.make_async_remote_copy(
            src_ref=kg_tot, dst_ref=out_g.at[me], send_sem=kt_send.at[j - 1], recv_sem=kt_rsem.at[j - 1],
            device_id={"seq": lax.rem(me + j, 4)}, device_id_type=MESH,
        )

    for j in range(1, n_dp):
        kg_copy(j).start()

    grad_t = jnp.transpose(o_a[FG].astype(F32))
    key_t = jnp.transpose(x_a[K].astype(F32)).astype(BF)
    query = x_a[Q] * jnp.asarray(0.125, BF)
    scaled = [(grad_t[64 * h : 64 * h + 64] * r_scr[h, 0:1, :]).astype(BF) for h in range(2)]
    grad = jnp.transpose(stack(*scaled).astype(F32)).astype(BF)
    blank = jnp.zeros((64, span), BF)
    dq_t, dk, dv = [], 0.0, 0.0
    for h in range(2):
        delta = jnp.sum(scaled[h].astype(F32) * att_t[h], axis=0, keepdims=True)
        masked_t = stack(scaled[h], blank) if h == 0 else stack(blank, scaled[h])
        one, two, three = backward(
            h, x_a.at[V], masked_t, pick(grad, h), pick(query, h), key_t[64 * h : 64 * h + 64], delta
        )
        dq_t.append(one)
        dk = dk + two
        dv = dv + three
    o_a[DQ] = (jnp.transpose(stack(*dq_t)) * 0.125).astype(BF)
    o_a[DK] = dk.astype(BF)
    o_a[DV] = dv.astype(BF)
    for n in (DQ, DK, DV):
        give_a(n)

    for j in range(1, n_dp):
        kg_copy(j).wait_recv()
    total = kg_recv[0]
    for d in range(1, n_dp):
        total = total + kg_recv[d]
    kg_tot[...] = total * (1.0 / n_dp)
    out_g[me] = kg_tot[...]
    for j in range(1, 4):
        kt_copy(j).start()

    grad_t = jnp.transpose(stack(u_b[:, :64], u_b[:, 64:]).astype(F32))
    key_t = jnp.transpose(k_b[...].astype(F32)).astype(BF)
    query_b = q_b[...] * jnp.asarray(0.125, BF)
    scaled_b = (grad_t * r_scr[2, 0:1, :]).astype(BF)
    delta = jnp.sum(scaled_b.astype(F32) * att_t[2], axis=0, keepdims=True)
    grad = jnp.transpose(scaled_b.astype(F32)).astype(BF)
    one, two, three = backward(2, v_b, scaled_b, grad, query_b, key_t, delta)
    for n, whole in ((DQ, jnp.transpose(one) * 0.125), (DK, two), (DV, three)):
        whole = whole.astype(BF)
        for d in range(4):
            o_b[n, d] = side(whole[d * rows : d * rows + half], whole[d * rows + half : (d + 1) * rows])
        give_b(n)

    for n in range(5):
        for part in range(2):
            each(in_copy, n, part, "send")
            each(back_copy, n, part, "send")
            each(back_copy, n, part, "recv")
    for j in range(1, n_dp):
        kg_copy(j).wait_send()
    for j in range(1, 4):
        kt_copy(j).wait_send()
        kt_copy(j).wait_recv()


def spread_kernel(a_ref, b_ref, g_ref, *outs):
    half = b_ref.shape[2]
    for n in range(5):
        for d in range(4):
            outs[n][:, 128 * d : 128 * d + 128] = a_ref[n, d]
        for d in range(2):
            lo, hi = b_ref[n, 2 * d], b_ref[n, 2 * d + 1]
            lanes = slice(512 + 128 * d, 640 + 128 * d)
            outs[n][0:half, lanes] = side(lo[:, :64], hi[:, :64])
            outs[n][half : 2 * half, lanes] = side(lo[:, 64:], hi[:, 64:])
    for d in range(4):
        outs[5][:, 128 * d : 128 * d + 128] = g_ref[d, 0]
    for d in range(2):
        outs[5][:, 512 + 128 * d : 640 + 128 * d] = side(g_ref[2 * d, 1][:, :64], g_ref[2 * d + 1, 1][:, :64])


def by_heads(n_dp, queries, keys, values, frames, upstream, lengths, conv_kernel):
    rows, channels = queries.shape
    half, span = rows // 2, 4 * rows
    mid = span // 2
    vm = pltpu.VMEM
    whole = pl.BlockSpec(memory_space=pltpu.VMEM)
    dma = pltpu.SemaphoreType.DMA
    out_a, out_b, out_g = pl.pallas_call(
        functools.partial(main_kernel, n_dp),
        name="heads",
        out_shape=(
            jax.ShapeDtypeStruct((5, 4, rows, 128), BF),
            jax.ShapeDtypeStruct((5, 4, half, 128), BF),
            jax.ShapeDtypeStruct((4, 2, KERNEL, 128), F32),
        ),
        in_specs=[pl.BlockSpec(memory_space=pltpu.SMEM)] + [whole] * 6,
        out_specs=(whole, whole, whole),
        scratch_shapes=[
            vm((5, 4, rows, 128), BF),
            vm((5, 4, half, 128), BF),
            vm((5, span, 128), BF),
            vm((5, 4, half, 128), BF),
            vm((span, 64), BF),
            vm((span, 64), BF),
            vm((span, 64), BF),
            vm((mid, 128), BF),
            vm((mid, 128), BF),
            vm((5, span, 128), BF),
            vm((5, 4, half, 128), BF),
            vm((3, span, span), BF),
            vm((span, span), F32),
            vm((span, span), BF),
            vm((3, 64, span), F32),
            vm((3, 8, span), F32),
            vm((2, span, 128), F32),
            vm((span + 32, 128), F32),
            vm((mid + 32, 128), F32),
            vm((span + 32, 128), F32),
            vm((mid + 32, 128), F32),
            vm((2, KERNEL, 128), F32),
            vm((2, KERNEL, 8, 128), F32),
            vm((2, KERNEL, 128), F32),
            vm((n_dp, 2, KERNEL, 128), F32),
            vm((2, KERNEL, 128), F32),
            dma((5, 2, 3)),
            dma((5, 2, 3)),
            dma((5, 2, 3)),
            dma((5, 2, 3)),
            dma((n_dp - 1,)),
            dma((n_dp - 1,)),
            dma((3,)),
            dma((3,)),
        ],
        compiler_params=pltpu.CompilerParams(
            collective_id=0, has_side_effects=True, vmem_limit_bytes=40 * 1024 * 1024
        ),
        cost_estimate=pl.CostEstimate(
            flops=10 * 12 * rows * span * 64, bytes_accessed=10 * rows * channels * 2, transcendentals=12 * rows * span
        ),
    )(lengths, queries, keys, values, frames, upstream, conv_kernel)
    flat = jax.ShapeDtypeStruct((rows, channels), BF)
    parts = pl.pallas_call(
        spread_kernel,
        name="spread",
        out_shape=(flat,) * 5 + (jax.ShapeDtypeStruct((KERNEL, channels), F32),),
        in_specs=[whole] * 3,
        out_specs=(whole,) * 6,
        compiler_params=pltpu.CompilerParams(vmem_limit_bytes=32 * 1024 * 1024),
    )(out_a, out_b, out_g)
    out, frame_grad, query_grad, key_grad, value_grad, kernel_grad = parts
    return out, query_grad, key_grad, value_grad, frame_grad, kernel_grad


def solution(mesh):
    placed = (
        P(("dp", "seq"), None),
        P(("dp", "seq"), None),
        P(("dp", "seq"), None),
        P(("dp", "seq"), None),
        P(("dp", "seq"), None),
        P("dp"),
        P(),
    )
    def body(*arrays):
        rows, channels = arrays[0].shape
        if mesh.shape["seq"] == 4 and channels == 12 * HEAD_DIM and rows == 160 and mesh.shape["dp"] > 1:
            return by_heads(mesh.shape["dp"], *arrays)
        return per_device(*arrays)

    return jax.shard_map(
        body,
        mesh=mesh,
        in_specs=placed,
        out_specs=(
            P(("dp", "seq"), None),
            P(("dp", "seq"), None),
            P(("dp", "seq"), None),
            P(("dp", "seq"), None),
            P(("dp", "seq"), None),
            P(),
        ),
        check_vma=False,
    )
```
